256 devices in a mesh: row: 16 (over y, x), col: 8 (over z), dp: 2 (over core).
Axes of the slice: x: 4, y: 4, z: 8, core: 2. Of those that a mesh axis runs over, the one named last changes fastest.
Arguments:
- tokens_in: bfloat16 [4096, 6144], P(('dp', 'col'), 'row'), parts along dimension 0, may hold values from -14 to 14, as said below
- norm_gain_vector: float32 [6144], P('row'), may hold values from 0.5 to 1.5
- w_in: bfloat16 [6144, 12288], P('row', 'col'), may hold values from -0.078125 to 0.078125
- w_out: bfloat16 [12288, 6144], P('col', 'row'), may hold values from -0.0546875 to 0.0546875
- cotangent: bfloat16 [4096, 6144], P(('dp', 'col'), 'row'), parts along dimension 0, may hold values from -6 to 6
Outputs:
- block_out: bfloat16 [4096, 6144], P(('dp', 'col'), 'row'), parts along dimension 0
- input_gradient: bfloat16 [4096, 6144], P(('dp', 'col'), 'row'), parts along dimension 0
- grad_w_in: bfloat16 [6144, 24576], P('row', ('dp', 'col')), parts along dimension 1
- grad_w_out: bfloat16 [12288, 12288], P('col', ('dp', 'row')), parts along dimension 1
The draws below stay inside these ranges and needn't reach their ends.
There are 2 independent parts, one for each index of `dp`. The reference program is written for one: setup_inputs(seed, part) draws one part's arguments, and reference() takes and returns one part's arrays. A program takes and returns all parts, laid end to end along the dimension named above; an argument that names none is the same for every part. Nothing has to cross between parts.
Inputs may be any that keep to these rules, and one draw needn't show every extreme that they name: `tokens_in`: features of a token.
All inputs are finite; a program needn't handle non-finite values.
Results may differ from the reference program's by a relative error of at most 0.018.
Values may be sent and summed in bfloat16 or wider, within the bound.
No kernel may reach another device: no remote copies, remote signals or barrier semaphores. Data moves between devices by JAX's collectives and lax.ppermute only.
A program may use at most 128 MiB of HBM per device.

```python
import math
import jax
import jax.numpy as jnp
from jax import lax

D = 6144
FF = 12288
TOKENS = 2048
N_ROW = 16
N_COL = 8


def draw_tokens_in(key, part):
    key = jax.random.fold_in(key, 11)
    key_col, key_off, key_base, key_tok = jax.random.split(key, 4)
    position = jnp.arange(D, dtype=jnp.float32) / D
    column = jnp.exp(position * math.log(3.0)) * jnp.exp(jax.random.uniform(key_col, (D,), jnp.float32, 0.0, math.log(10.0 / 3.0)))
    offset = jnp.clip(0.5 * jax.random.normal(key_off, (D,), jnp.float32), -1.5, 1.5)
    token_shift = jnp.clip(1.5 * jax.random.normal(key_tok, (TOKENS,), jnp.float32), -4.0, 4.0)
    base = jnp.clip(jax.random.normal(key_base, (TOKENS, D), jnp.float32), -3.5, 3.5)
    values = base * column[None, :] * 0.33 + offset[None, :] + token_shift[:, None]
    return jnp.clip(values, -14.0, 14.0).astype(jnp.bfloat16)


def draw_w_in(key, part):
    key = jax.random.fold_in(key, 23)
    key_base, key_shared = jax.random.split(key, 2)
    scale = 1.0 / math.sqrt(D)
    base = jnp.clip(jax.random.normal(key_base, (D, FF), jnp.float32), -4.0, 4.0) * scale
    shared = jnp.clip(0.6 * jax.random.normal(key_shared, (FF,), jnp.float32), -1.8, 1.8) * scale
    return jnp.clip(base + shared[None, :], -0.078125, 0.078125).astype(jnp.bfloat16)


def block_scale(rng, dims, pieces, smallest, largest):
    def one(dim, blocks):
        draws = jax.random.uniform(jax.random.fold_in(jax.random.fold_in(rng, 6), dim), (blocks,), jnp.float32, smallest / len(pieces), largest / len(pieces))
        return jnp.repeat(jnp.exp(draws), dims[dim] // blocks).reshape((-1,) + (1,) * (len(dims) - dim - 1))

    level = one(*pieces[0])
    for cut in pieces[1:]:
        level = level * one(*cut)
    return level


def noise(own_key, dims, deviation, most, cuts=(), kind=jnp.bfloat16):
    factor_of = block_scale(own_key, dims, cuts, -0.22, 0.18) if cuts else 1.0
    array = jax.random.normal(own_key, dims, jnp.float32) * deviation * factor_of
    return jnp.minimum(jnp.maximum(array, -most), most).astype(kind)


def setup_inputs(seed: int = 0, part: int = 0) -> dict:
    key_list = jax.random.split(jax.random.key(seed), 6)
    part_splits = jax.random.split(jax.random.fold_in(key_list[5], part), 6)
    tokens_in = draw_tokens_in(jax.random.fold_in(jax.random.fold_in(key_list[5], part), 71), part)
    norm_gain_vector = jnp.clip(0.5 + 1.0 * jax.random.uniform(key_list[1], (D,), jnp.float32) ** block_scale(key_list[1], (D,), ((0, 16),), -0.2, 0.2), 0.5, 1.5)
    w_in = draw_w_in(jax.random.fold_in(key_list[5], 71), part)
    w_out = noise(key_list[3], (FF, D), FF ** -0.5, 0.0546875, ((0, 8), (1, 16)))
    cotangent = noise(part_splits[4], (TOKENS, D), 1.0, 6.0, ((0, 8), (1, 16)))
    return {"tokens_in": tokens_in, "norm_gain_vector": norm_gain_vector, "w_in": w_in, "w_out": w_out, "cotangent": cotangent}


EPS = 1e-06
GELU_C = 0.7978845608028654

def gelu_value(pre):
    inner = GELU_C * (pre + 0.044715 * pre * pre * pre)
    return 0.5 * pre * (1.0 + jnp.tanh(inner))

def gelu_slope(pre):
    inner = GELU_C * (pre + 0.044715 * pre * pre * pre)
    tangent = jnp.tanh(inner)
    return 0.5 * (1.0 + tangent) + 0.5 * pre * (1.0 - tangent * tangent) * GELU_C * (1.0 + 3.0 * 0.044715 * pre * pre)

def blocked_product(left, right, blocks):
    width = left.shape[1] // blocks
    total = jnp.zeros((left.shape[0], right.shape[1]), jnp.float32)
    for index in range(blocks):
        piece = jnp.dot(left[:, index * width:(index + 1) * width], right[index * width:(index + 1) * width], preferred_element_type=jnp.float32)
        rounded = lax.optimization_barrier(piece.astype(jnp.bfloat16))
        total = total + rounded.astype(jnp.float32)
    return total

def reference(tokens_in, norm_gain_vector, w_in, w_out, cotangent):
    input_complete = tokens_in.astype(jnp.float32)
    row_average = lax.optimization_barrier(jnp.mean(input_complete, axis=1, keepdims=True))
    meansq = lax.optimization_barrier(jnp.mean(input_complete * input_complete, axis=1, keepdims=True))
    inverse_deviation = lax.rsqrt(meansq - row_average * row_average + EPS)
    centered_normalized = (input_complete - row_average) * inverse_deviation
    normed_tokens = (centered_normalized * norm_gain_vector[None, :]).astype(jnp.bfloat16)
    pre = blocked_product(normed_tokens, w_in, N_ROW)
    act = gelu_value(pre).astype(jnp.bfloat16)
    block_out = (input_complete + blocked_product(act, w_out, N_COL)).astype(jnp.bfloat16)
    d_act = blocked_product(cotangent, w_out.T, N_ROW)
    d_pre = (d_act * gelu_slope(pre)).astype(jnp.bfloat16)
    grad_w_out = jnp.dot(act.T, cotangent, preferred_element_type=jnp.float32).astype(jnp.bfloat16)
    grad_w_in = jnp.dot(normed_tokens.T, d_pre, preferred_element_type=jnp.float32).astype(jnp.bfloat16)
    d_normed = blocked_product(d_pre, w_in.T, N_COL)
    scaled_tokens = d_normed * norm_gain_vector[None, :]
    first_matmul = lax.optimization_barrier(jnp.mean(scaled_tokens, axis=1, keepdims=True))
    second_matmul = lax.optimization_barrier(jnp.mean(scaled_tokens * centered_normalized, axis=1, keepdims=True))
    input_gradient = (cotangent.astype(jnp.float32) + inverse_deviation * (scaled_tokens - first_matmul - centered_normalized * second_matmul)).astype(jnp.bfloat16)
    return (block_out, input_gradient, grad_w_in, grad_w_out)
```

```python
import functools

import jax
import jax.numpy as jnp
from jax import lax
from jax.experimental import pallas as pl
from jax.experimental.pallas import tpu as pltpu
from jax.sharding import PartitionSpec as P

EPS = 1e-06
GELU_C = 0.7978845608028654
RING = 4
DEPTH = 8
BF16 = jnp.bfloat16
F32 = jnp.float32


def gelu_value(pre):
    inner = GELU_C * (pre + 0.044715 * pre * pre * pre)
    return 0.5 * pre * (1.0 + jnp.tanh(inner))


def gelu_slope(pre):
    inner = GELU_C * (pre + 0.044715 * pre * pre * pre)
    tangent = jnp.tanh(inner)
    return 0.5 * (1.0 + tangent) + 0.5 * pre * (1.0 - tangent * tangent) * GELU_C * (
        1.0 + 3.0 * 0.044715 * pre * pre
    )


def dot(left, right, left_dim, right_dim):
    return lax.dot_general(
        left, right, (((left_dim,), (right_dim,)), ((), ())), preferred_element_type=F32
    )


def receive(value, axis, offset):
    if axis == "core":
        return lax.ppermute(value, "dp", [(0, 1), (1, 0)])
    pairs = []
    for core, step in ((0, offset), (1, -offset)):
        if axis == "z":
            pairs += [(2 * ((i + step) % DEPTH) + core, 2 * i + core) for i in range(DEPTH)]
            continue
        for y in range(RING):
            for x in range(RING):
                if axis == "x":
                    source = RING * y + (x + step) % RING
                else:
                    source = RING * ((y + step) % RING) + x
                pairs.append((2 * source + core, 2 * (RING * y + x) + core))
    return lax.ppermute(value, ("col" if axis == "z" else "row", "dp"), pairs)


def phase(*moves, after=()):
    values = lax.optimization_barrier(tuple(move[0] for move in moves) + tuple(after))
    return [receive(value, axis, offset) for value, (_, axis, offset) in zip(values, moves)]


def phase_and(moves, seen):
    values = lax.optimization_barrier(tuple(move[0] for move in moves) + tuple(seen))
    moved = [receive(value, axis, offset) for value, (_, axis, offset) in zip(values, moves)]
    return moved + list(values[len(moves) :])


def add_up(values):
    total = values[0].astype(F32)
    for value in values[1:]:
        total = total + value.astype(F32)
    return total


def split3(value):
    high = lax.reduce_precision(value, 8, 7)
    middle = lax.reduce_precision(value - high, 8, 7)
    return [part.astype(BF16) for part in (high, middle, value - high - middle)]


def with_row(piece, row):
    filler = jnp.zeros((16 - row.shape[0], row.shape[1]), BF16)
    return jnp.concatenate([piece, row, filler], axis=0)


def sum_columns(first, second):
    lane = lax.broadcasted_iota(jnp.int32, (first.shape[0], 128), 1)
    extra = jnp.zeros(lane.shape, F32)
    for index, part in enumerate(split3(first) + split3(second)):
        extra = jnp.where(lane == index, part.astype(F32), extra)
    return extra.astype(BF16)


def total_sums(columns_per_device, group):
    first, second = 0.0, 0.0
    for o, extra in enumerate(columns_per_device):
        parts = [extra[:, i : i + 1].astype(F32) for i in range(6)]
        one, two = parts[0] + parts[1] + parts[2], parts[3] + parts[4] + parts[5]
        if o:
            one = jnp.concatenate([one[-o * group :], one[: -o * group]], axis=0)
            two = jnp.concatenate([two[-o * group :], two[: -o * group]], axis=0)
        first, second = first + one, second + two
    return first, second


def small_call(body, outputs, *inputs):
    return pl.pallas_call(
        body,
        out_shape=[jax.ShapeDtypeStruct(shape, dtype) for shape, dtype in outputs],
        in_specs=[pl.BlockSpec(memory_space=pltpu.VMEM)] * len(inputs),
        out_specs=[pl.BlockSpec(memory_space=pltpu.VMEM)] * len(outputs),
        compiler_params=pltpu.CompilerParams(vmem_limit_bytes=32 * 1024 * 1024),
    )(*inputs)


def forward_sums(x0, x1, x2, x3, g0, g1, g2, g3, own, gain, s0, s1, s2, s3):
    count, width = g0.shape
    first, second = 0.0, 0.0
    for o, piece in enumerate((x0, x1, x2, x3)):
        block = piece[:count, :]
        own[:, o * width : (o + 1) * width] = block
        rows = piece[count : count + 16, :].astype(F32)
        gain[:, o * width : (o + 1) * width] = rows[0:1] + rows[1:2] + rows[2:3]
        block = block.astype(F32)
        first = first + jnp.sum(block, axis=1, keepdims=True)
        second = second + jnp.sum(block * block, axis=1, keepdims=True)
    extra = sum_columns(first, second)
    for piece, sent in zip((g0, g1, g2, g3), (s0, s1, s2, s3)):
        sent[:, :width] = piece[...]
        sent[:, width:] = extra


def forward_norm(features, group, own, gain, r0, r1, r2, r3, both, stats):
    count, width = own.shape[0], own.shape[1] // RING
    received = (r0, r1, r2, r3)
    first, second = total_sums([piece[:, width:] for piece in received], group)
    mean = first / features
    rstd = lax.rsqrt(second / features - mean * mean + EPS)
    lane = lax.broadcasted_iota(jnp.int32, (count, 128), 1)
    stats[...] = jnp.where(lane == 0, mean, rstd)
    both[:count, :] = ((own[...].astype(F32) - mean) * rstd * gain[...]).astype(BF16)
    for o, piece in enumerate(received):
        both[count:, o * width : (o + 1) * width] = piece[:, :width]


def backward_sums(part, up, down, own, gain, stats, scaled, s0, s1, s2, s3):
    count, width = own.shape[0], own.shape[1] // RING

    def total(rows):
        return part[rows, :].astype(F32) + up[rows, :].astype(F32) + down[rows, :].astype(F32)

    value = total(slice(0, count)) * gain[...]
    scaled[...] = value
    xhat = (own[...].astype(F32) - stats[:, 0:1]) * stats[:, 1:2]
    extra = sum_columns(
        jnp.sum(value, axis=1, keepdims=True), jnp.sum(value * xhat, axis=1, keepdims=True)
    )
    block = total(slice(count, 2 * count)).astype(BF16)
    for o, sent in enumerate((s0, s1, s2, s3)):
        sent[:, :width] = block[:, o * width : (o + 1) * width]
        sent[:, width:] = extra


def backward_norm(features, group, scaled, own, stats, r0, r1, r2, r3, t0, t1, t2, t3):
    width = own.shape[1] // RING
    first, second = total_sums([piece[:, width:] for piece in (r0, r1, r2, r3)], group)
    mean, rstd = stats[:, 0:1], stats[:, 1:2]
    for o, through in enumerate((t0, t1, t2, t3)):
        at = slice(o * width, (o + 1) * width)
        xhat = (own[:, at].astype(F32) - mean) * rstd
        value = scaled[:, at] - first / features - xhat * (second / features)
        through[...] = (rstd * value).astype(BF16)


def exchange4(pieces, axis, after=()):
    first, third, second = lax.optimization_barrier(
        tuple(phase(*[(pieces[RING - o], axis, o) for o in (1, 3, 2)], after=after))
    )
    return [pieces[0], first, second, third]


def rotate(value, axis, start):
    doubled = jnp.concatenate([value, value], axis=axis)
    return lax.dynamic_slice_in_dim(doubled, start, value.shape[axis], axis=axis)


def columns(value, index, width=384):
    return value[:, index * width : (index + 1) * width]


def shards(tokens_in, norm_gain_vector, w_in, w_out, cotangent):
    row = lax.axis_index("row")
    x_at, y_at, core = row % RING, row // RING, lax.axis_index("dp")
    width = tokens_in.shape[1]
    features = width * RING * RING
    group = tokens_in.shape[0] // 16
    rows = DEPTH * group

    x_start = jnp.where(core == 0, x_at, RING - 1 - x_at)
    y_start = jnp.where(core == 0, y_at, RING - 1 - y_at)
    x_back = jnp.where(core == 0, (RING - x_at) % RING, RING - 1 - x_at)
    y_back = jnp.where(core == 0, (RING - y_at) % RING, RING - 1 - y_at)

    def mirrored(value):
        return jnp.where(core == 0, value, value[::-1, ::-1])

    def to_relative(value):
        value = mirrored(value.reshape(RING, RING, group, width))
        return rotate(rotate(value, 0, x_start), 1, y_start)

    def from_relative(value):
        value = rotate(rotate(mirrored(value), 0, x_back), 1, y_back)
        return value.reshape(RING * RING * group, width)

    tokens = to_relative(tokens_in)
    grads = to_relative(cotangent)
    gain_rows = jnp.stack(split3(norm_gain_vector))
    arrived = exchange4(
        [with_row(tokens[o].reshape(RING * group, width), gain_rows) for o in range(RING)], "x"
    )
    count, wide = RING * group, RING * width
    pieces = [grads[:, o].reshape(count, width) for o in range(RING)]
    own, gain, *pieces = small_call(
        forward_sums,
        [((count, wide), BF16), ((1, wide), F32)] + [((count, width + 128), BF16)] * RING,
        *arrived,
        *pieces,
    )
    arrived = exchange4(pieces, "y")
    both, stats = small_call(
        functools.partial(forward_norm, features, group),
        [((2 * count, wide), BF16), ((count, 128), F32)],
        own,
        gain,
        *arrived,
    )

    gathered = [both] + [None] * (DEPTH - 1)
    in_up, out_up, up, down = phase(
        (w_in, "x", 1), (w_out, "y", 1), (both, "z", 1), (both, "z", -1)
    )
    gathered[1], gathered[7] = up, down
    up, down = phase((up, "z", 1), (down, "z", -1))
    gathered[2], gathered[6] = up, down
    up, down, in_up, out_up = lax.optimization_barrier((up, down, in_up, out_up))
    half = w_in.shape[0] // 2
    in_half = lax.dynamic_slice_in_dim(in_up, core * half, half, axis=0)
    half = w_out.shape[0] // 2
    out_half = lax.dynamic_slice_in_dim(out_up, core * half, half, axis=0)
    in_half, out_half, up, down = phase(
        (in_half, "x", 1), (out_half, "y", 1), (up, "z", 1), (down, "z", -1)
    )
    gathered[3], gathered[5] = up, down
    in_half, out_half, up = lax.optimization_barrier((in_half, out_half, up))
    in_down, out_down, in_far, out_far, gathered[4] = phase(
        (in_up, "core", 1),
        (out_up, "core", 1),
        (in_half, "core", 1),
        (out_half, "core", 1),
        (up, "z", 1),
    )

    def panel_of(pieces):
        stacked = jnp.stack([piece.reshape(RING, group, wide) for piece in pieces], axis=1)
        return stacked.reshape(RING * rows, wide)

    normed = panel_of([piece[:count] for piece in gathered])
    grad_panel = panel_of([piece[count:] for piece in gathered])

    def panel_of_weights(block, up, half, down, far, stack):
        block, up = lax.optimization_barrier((block, up))
        size, rows_half = block.shape[stack], half.shape[0]
        shape = [block.shape[0], block.shape[1]]
        shape[stack] *= RING
        panel = jnp.zeros(shape, block.dtype)
        for o, piece, row in (
            (0, block, 0),
            (1, up, 0),
            (2, half, core * rows_half),
            (3, down, 0),
            (2, far, (1 - core) * rows_half),
        ):
            at = (row + o * size, 0) if stack == 0 else (row, o * size)
            panel = lax.dynamic_update_slice(panel, piece, at)
        return panel

    in_panel = panel_of_weights(w_in, in_up, in_half, in_down, in_far, 0)
    out_panel = panel_of_weights(w_out, out_up, out_half, out_down, out_far, 1)
    in_panel, normed = lax.optimization_barrier((in_panel, normed))
    out_panel, grad_panel = lax.optimization_barrier((out_panel, grad_panel))

    def by_group(part):
        return [part[o * rows : (o + 1) * rows] for o in range(RING)]

    pre_shares = by_group(dot(normed, in_panel, 1, 0).astype(BF16))
    d_shares = by_group(dot(grad_panel, out_panel, 1, 1).astype(BF16))
    pre = add_up(exchange4(pre_shares, "y"))
    d_parts = exchange4(d_shares, "x")
    act, pre = lax.optimization_barrier((gelu_value(pre).astype(BF16), pre))
    act_parts = phase((act, "x", 1), (act, "x", 2), (act, "x", 3))
    d_pre = (add_up(d_parts) * gelu_slope(pre)).astype(BF16)
    d_panel = jnp.concatenate(exchange4([d_pre] * RING, "y"), axis=0)
    act_panel = jnp.concatenate([act, *act_parts], axis=0)

    in_far = dot(columns(normed, 2), d_panel, 0, 0).astype(BF16)
    out_far = dot(act_panel, columns(grad_panel, 2), 0, 0).astype(BF16)
    in_up, out_up = phase((in_far, "x", -1), (out_far, "y", -1))
    d_panel, act_panel, in_far, out_far = lax.optimization_barrier(
        (d_panel, act_panel, in_far, out_far)
    )
    dn_part = dot(d_panel, in_panel, 1, 1).astype(BF16).reshape(RING, DEPTH, group, wide)
    out_part = dot(act_panel, out_panel, 1, 0).astype(BF16).reshape(RING, DEPTH, group, wide)

    def part(o):
        return jnp.concatenate(
            [dn_part[:, o].reshape(count, wide), out_part[:, o].reshape(count, wide)], axis=0
        )

    up, down = phase((part(4), "z", -1), (part(5), "z", 1))
    up, down, d_panel, act_panel = lax.optimization_barrier((up, down, d_panel, act_panel))
    in_ahead, in_back = (dot(columns(normed, o), d_panel, 0, 0).astype(BF16) for o in (1, 3))
    out_ahead, out_back = (
        dot(act_panel, columns(grad_panel, o), 0, 0).astype(BF16) for o in (1, 3)
    )
    in_ahead, in_back, out_ahead, out_back = lax.optimization_barrier(
        (in_ahead, in_back, out_ahead, out_back)
    )
    up, down = phase((part(3) + up, "z", -1), (part(6) + down, "z", 1))
    up, down, in_up, out_up = lax.optimization_barrier((up, down, in_up, out_up))
    in_up, in_down, out_up, up, down = phase(
        (in_ahead + in_up, "x", -1),
        (in_back, "x", 1),
        (out_ahead + out_up, "y", -1),
        (part(2) + up, "z", -1),
        (part(7) + down, "z", 1),
    )
    up, down, d_panel, act_panel, out_back = lax.optimization_barrier(
        (up, down, d_panel, act_panel, out_back)
    )
    in_own = dot(columns(normed, 0), d_panel, 0, 0).astype(BF16)
    out_own = dot(act_panel, columns(grad_panel, 0), 0, 0).astype(BF16)
    (out_down,) = phase((out_back, "y", 1))
    (up,) = phase((part(1) + up, "z", -1))
    up, down, in_up, out_up, in_down, out_down, in_own, out_own = lax.optimization_barrier(
        (up, down, in_up, out_up, in_down, out_down, in_own, out_own)
    )
    scaled, *pieces = small_call(
        backward_sums,
        [((count, wide), F32)] + [((count, width + 128), BF16)] * RING,
        part(0),
        up,
        down,
        own,
        gain,
        stats,
    )
    arrived = exchange4(pieces, "y")
    scaled, out_own, out_up, out_down = lax.optimization_barrier(
        (scaled, out_own, out_up, out_down)
    )
    grad_w_out = add_up((out_own, out_up, out_down)).astype(BF16)
    through = small_call(
        functools.partial(backward_norm, features, group),
        [((count, width), BF16)] * RING,
        scaled,
        own,
        stats,
        *arrived,
    )
    *through, in_own, in_up, in_down = lax.optimization_barrier(
        (*through, in_own, in_up, in_down)
    )
    grad_w_in = add_up((in_own, in_up, in_down)).astype(BF16)
    through = exchange4(through, "x")
    through = jnp.stack([piece.reshape(RING, group, width) for piece in through], axis=0)
    input_gradient = (cotangent.astype(F32) + from_relative(through).astype(F32)).astype(BF16)
    block = jnp.stack([piece[:, :width].reshape(RING, group, width) for piece in arrived], axis=1)
    block_out = (tokens_in.astype(F32) + from_relative(block).astype(F32)).astype(BF16)
    return block_out, input_gradient, grad_w_in, grad_w_out


def solution(mesh):
    return jax.shard_map(
        shards,
        mesh=mesh,
        in_specs=(
            P(("dp", "col"), "row"),
            P("row"),
            P("row", "col"),
            P("col", "row"),
            P(("dp", "col"), "row"),
        ),
        out_specs=(
            P(("dp", "col"), "row"),
            P(("dp", "col"), "row"),
            P("row", ("dp", "col")),
            P("col", ("dp", "row")),
        ),
        check_vma=False,
    )
```

```python
import functools

import jax
import jax.numpy as jnp
from jax import lax
from jax.experimental import pallas as pl
from jax.experimental.pallas import tpu as pltpu
from jax.sharding import PartitionSpec as P

EPS = 1e-06
GELU_C = 0.7978845608028654
RING = 4
DEPTH = 8
BF16 = jnp.bfloat16
F32 = jnp.float32


def gelu_value(pre):
    inner = GELU_C * (pre + 0.044715 * pre * pre * pre)
    return 0.5 * pre * (1.0 + jnp.tanh(inner))


def gelu_slope(pre):
    inner = GELU_C * (pre + 0.044715 * pre * pre * pre)
    tangent = jnp.tanh(inner)
    return 0.5 * (1.0 + tangent) + 0.5 * pre * (1.0 - tangent * tangent) * GELU_C * (
        1.0 + 3.0 * 0.044715 * pre * pre
    )


def dot(left, right, left_dim, right_dim):
    return lax.dot_general(
        left, right, (((left_dim,), (right_dim,)), ((), ())), preferred_element_type=F32
    )


def receive(value, axis, offset):
    if axis == "core":
        return lax.ppermute(value, "dp", [(0, 1), (1, 0)])
    pairs = []
    for core, step in ((0, offset), (1, -offset)):
        if axis == "z":
            pairs += [(2 * ((i + step) % DEPTH) + core, 2 * i + core) for i in range(DEPTH)]
            continue
        for y in range(RING):
            for x in range(RING):
                if axis == "x":
                    source = RING * y + (x + step) % RING
                else:
                    source = RING * ((y + step) % RING) + x
                pairs.append((2 * source + core, 2 * (RING * y + x) + core))
    return lax.ppermute(value, ("col" if axis == "z" else "row", "dp"), pairs)


def phase(*moves, after=()):
    values = lax.optimization_barrier(tuple(move[0] for move in moves) + tuple(after))
    return [receive(value, axis, offset) for value, (_, axis, offset) in zip(values, moves)]


def phase_and(moves, seen):
    values = lax.optimization_barrier(tuple(move[0] for move in moves) + tuple(seen))
    moved = [receive(value, axis, offset) for value, (_, axis, offset) in zip(values, moves)]
    return moved + list(values[len(moves) :])


def add_up(values):
    total = values[0].astype(F32)
    for value in values[1:]:
        total = total + value.astype(F32)
    return total


def split3(value):
    high = lax.reduce_precision(value, 8, 7)
    middle = lax.reduce_precision(value - high, 8, 7)
    return [part.astype(BF16) for part in (high, middle, value - high - middle)]


def with_row(piece, row):
    filler = jnp.zeros((16 - row.shape[0], row.shape[1]), BF16)
    return jnp.concatenate([piece, row, filler], axis=0)


def sum_columns(first, second):
    lane = lax.broadcasted_iota(jnp.int32, (first.shape[0], 128), 1)
    extra = jnp.zeros(lane.shape, F32)
    for index, part in enumerate(split3(first) + split3(second)):
        extra = jnp.where(lane == index, part.astype(F32), extra)
    return extra.astype(BF16)


def total_sums(columns_per_device, group):
    first, second = 0.0, 0.0
    for o, extra in enumerate(columns_per_device):
        parts = [extra[:, i : i + 1].astype(F32) for i in range(6)]
        one, two = parts[0] + parts[1] + parts[2], parts[3] + parts[4] + parts[5]
        if o:
            one = jnp.concatenate([one[-o * group :], one[: -o * group]], axis=0)
            two = jnp.concatenate([two[-o * group :], two[: -o * group]], axis=0)
        first, second = first + one, second + two
    return first, second


def small_call(body, outputs, *inputs):
    return pl.pallas_call(
        body,
        out_shape=[jax.ShapeDtypeStruct(shape, dtype) for shape, dtype in outputs],
        in_specs=[pl.BlockSpec(memory_space=pltpu.VMEM)] * len(inputs),
        out_specs=[pl.BlockSpec(memory_space=pltpu.VMEM)] * len(outputs),
        compiler_params=pltpu.CompilerParams(vmem_limit_bytes=32 * 1024 * 1024),
    )(*inputs)


def forward_sums(x0, x1, x2, x3, g0, g1, g2, g3, own, gain, s0, s1, s2, s3):
    count, width = g0.shape
    first, second = 0.0, 0.0
    for o, piece in enumerate((x0, x1, x2, x3)):
        block = piece[:count, :]
        own[:, o * width : (o + 1) * width] = block
        rows = piece[count : count + 16, :].astype(F32)
        gain[:, o * width : (o + 1) * width] = rows[0:1] + rows[1:2] + rows[2:3]
        block = block.astype(F32)
        first = first + jnp.sum(block, axis=1, keepdims=True)
        second = second + jnp.sum(block * block, axis=1, keepdims=True)
    extra = sum_columns(first, second)
    for piece, sent in zip((g0, g1, g2, g3), (s0, s1, s2, s3)):
        sent[:, :width] = piece[...]
        sent[:, width:] = extra


def forward_norm(features, group, own, gain, r0, r1, r2, r3, both, stats):
    count, width = own.shape[0], own.shape[1] // RING
    received = (r0, r1, r2, r3)
    first, second = total_sums([piece[:, width:] for piece in received], group)
    mean = first / features
    rstd = lax.rsqrt(second / features - mean * mean + EPS)
    lane = lax.broadcasted_iota(jnp.int32, (count, 128), 1)
    stats[...] = jnp.where(lane == 0, mean, rstd)
    both[:count, :] = ((own[...].astype(F32) - mean) * rstd * gain[...]).astype(BF16)
    for o, piece in enumerate(received):
        both[count:, o * width : (o + 1) * width] = piece[:, :width]


def backward_sums(part, up, down, own, gain, stats, scaled, s0, s1, s2, s3):
    count, width = own.shape[0], own.shape[1] // RING

    def total(rows):
        return part[rows, :].astype(F32) + up[rows, :].astype(F32) + down[rows, :].astype(F32)

    value = total(slice(0, count)) * gain[...]
    scaled[...] = value
    xhat = (own[...].astype(F32) - stats[:, 0:1]) * stats[:, 1:2]
    extra = sum_columns(
        jnp.sum(value, axis=1, keepdims=True), jnp.sum(value * xhat, axis=1, keepdims=True)
    )
    block = total(slice(count, 2 * count)).astype(BF16)
    for o, sent in enumerate((s0, s1, s2, s3)):
        sent[:, :width] = block[:, o * width : (o + 1) * width]
        sent[:, width:] = extra


def backward_norm(features, group, scaled, own, stats, r0, r1, r2, r3, t0, t1, t2, t3):
    width = own.shape[1] // RING
    first, second = total_sums([piece[:, width:] for piece in (r0, r1, r2, r3)], group)
    mean, rstd = stats[:, 0:1], stats[:, 1:2]
    for o, through in enumerate((t0, t1, t2, t3)):
        at = slice(o * width, (o + 1) * width)
        xhat = (own[:, at].astype(F32) - mean) * rstd
        value = scaled[:, at] - first / features - xhat * (second / features)
        through[...] = (rstd * value).astype(BF16)


def exchange4(pieces, axis, after=()):
    first, third, second = lax.optimization_barrier(
        tuple(phase(*[(pieces[RING - o], axis, o) for o in (1, 3, 2)], after=after))
    )
    return [pieces[0], first, second, third]


def rotate(value, axis, start):
    doubled = jnp.concatenate([value, value], axis=axis)
    return lax.dynamic_slice_in_dim(doubled, start, value.shape[axis], axis=axis)


def columns(value, index, width=384):
    return value[:, index * width : (index + 1) * width]


def shards(tokens_in, norm_gain_vector, w_in, w_out, cotangent):
    row = lax.axis_index("row")
    x_at, y_at, core = row % RING, row // RING, lax.axis_index("dp")
    width = tokens_in.shape[1]
    features = width * RING * RING
    group = tokens_in.shape[0] // 16
    rows = DEPTH * group

    x_start = jnp.where(core == 0, x_at, RING - 1 - x_at)
    y_start = jnp.where(core == 0, y_at, RING - 1 - y_at)
    x_back = jnp.where(core == 0, (RING - x_at) % RING, RING - 1 - x_at)
    y_back = jnp.where(core == 0, (RING - y_at) % RING, RING - 1 - y_at)

    def mirrored(value):
        return jnp.where(core == 0, value, value[::-1, ::-1])

    def to_relative(value):
        value = mirrored(value.reshape(RING, RING, group, width))
        return rotate(rotate(value, 0, x_start), 1, y_start)

    def from_relative(value):
        value = rotate(rotate(mirrored(value), 0, x_back), 1, y_back)
        return value.reshape(RING * RING * group, width)

    tokens = to_relative(tokens_in)
    grads = to_relative(cotangent)
    gain_rows = jnp.stack(split3(norm_gain_vector))
    arrived = exchange4(
        [with_row(tokens[o].reshape(RING * group, width), gain_rows) for o in range(RING)], "x"
    )
    count, wide = RING * group, RING * width
    pieces = [grads[:, o].reshape(count, width) for o in range(RING)]
    own, gain, *pieces = small_call(
        forward_sums,
        [((count, wide), BF16), ((1, wide), F32)] + [((count, width + 128), BF16)] * RING,
        *arrived,
        *pieces,
    )
    (in_up,) = phase((w_in, "x", 1), after=(own,))
    arrived = exchange4(pieces, "y")
    both, stats = small_call(
        functools.partial(forward_norm, features, group),
        [((2 * count, wide), BF16), ((count, 128), F32)],
        own,
        gain,
        *arrived,
    )

    gathered = [both] + [None] * (DEPTH - 1)
    up, down = phase((both, "z", 1), (both, "z", -1))
    (out_up,) = phase((w_out, "y", 1), after=(both,))
    gathered[1], gathered[7] = up, down
    up, down, in_up = lax.optimization_barrier((up, down, in_up))
    half = w_in.shape[0] // 2
    in_half = lax.dynamic_slice_in_dim(in_up, core * half, half, axis=0)
    (in_half,) = phase((in_half, "x", 1))
    up, down = phase((up, "z", 1), (down, "z", -1))
    gathered[2], gathered[6] = up, down
    up, down, in_half, out_up = lax.optimization_barrier((up, down, in_half, out_up))
    half = w_out.shape[0] // 2
    out_half = lax.dynamic_slice_in_dim(out_up, core * half, half, axis=0)
    (out_half,) = phase((out_half, "y", 1))
    up, down = phase((up, "z", 1), (down, "z", -1))
    gathered[3], gathered[5] = up, down
    in_down, in_far = phase((in_up, "core", 1), (in_half, "core", 1))
    out_half, up, in_down, in_far = lax.optimization_barrier((out_half, up, in_down, in_far))
    out_down, out_far, gathered[4] = phase(
        (out_up, "core", 1), (out_half, "core", 1), (up, "z", 1)
    )

    def panel_of(pieces):
        stacked = jnp.stack([piece.reshape(RING, group, wide) for piece in pieces], axis=1)
        return stacked.reshape(RING * rows, wide)

    normed = panel_of([piece[:count] for piece in gathered])
    grad_panel = panel_of([piece[count:] for piece in gathered])

    def panel_of_weights(block, up, half, down, far, stack):
        block, up = lax.optimization_barrier((block, up))
        size, rows_half = block.shape[stack], half.shape[0]
        shape = [block.shape[0], block.shape[1]]
        shape[stack] *= RING
        panel = jnp.zeros(shape, block.dtype)
        for o, piece, row in (
            (0, block, 0),
            (1, up, 0),
            (2, half, core * rows_half),
            (3, down, 0),
            (2, far, (1 - core) * rows_half),
        ):
            at = (row + o * size, 0) if stack == 0 else (row, o * size)
            panel = lax.dynamic_update_slice(panel, piece, at)
        return panel

    in_panel = panel_of_weights(w_in, in_up, in_half, in_down, in_far, 0)
    out_panel = panel_of_weights(w_out, out_up, out_half, out_down, out_far, 1)
    in_panel, normed = lax.optimization_barrier((in_panel, normed))
    out_panel, grad_panel = lax.optimization_barrier((out_panel, grad_panel))

    def by_group(part):
        return [part[o * rows : (o + 1) * rows] for o in range(RING)]

    pre_shares = by_group(dot(normed, in_panel, 1, 0).astype(BF16))
    pre_shares, out_panel = lax.optimization_barrier((pre_shares, out_panel))
    d_shares = by_group(dot(grad_panel, out_panel, 1, 1).astype(BF16))
    pre = add_up(exchange4(pre_shares, "y"))
    d_parts = exchange4(d_shares, "x")
    act, pre, *d_parts = lax.optimization_barrier((gelu_value(pre).astype(BF16), pre, *d_parts))
    act_parts = phase((act, "x", 1), (act, "x", 2), (act, "x", 3))
    d_pre = (add_up(d_parts) * gelu_slope(pre)).astype(BF16)
    d_panel = jnp.concatenate(exchange4([d_pre] * RING, "y"), axis=0)
    act_panel = jnp.concatenate([act, *act_parts], axis=0)

    in_far = dot(columns(normed, 2), d_panel, 0, 0).astype(BF16)
    out_far = dot(act_panel, columns(grad_panel, 2), 0, 0).astype(BF16)
    in_up, out_up = phase((in_far, "x", -1), (out_far, "y", -1))
    d_panel, act_panel, in_far, out_far = lax.optimization_barrier(
        (d_panel, act_panel, in_far, out_far)
    )
    dn_part = dot(d_panel, in_panel, 1, 1).astype(BF16).reshape(RING, DEPTH, group, wide)
    out_part = dot(act_panel, out_panel, 1, 0).astype(BF16).reshape(RING, DEPTH, group, wide)

    def part(o):
        return jnp.concatenate(
            [dn_part[:, o].reshape(count, wide), out_part[:, o].reshape(count, wide)], axis=0
        )

    up, down = phase((part(4), "z", -1), (part(5), "z", 1))
    up, down, in_up, out_up, d_panel, act_panel = lax.optimization_barrier(
        (up, down, in_up, out_up, d_panel, act_panel)
    )
    in_ahead, in_back = (dot(columns(normed, o), d_panel, 0, 0).astype(BF16) for o in (1, 3))
    out_ahead, out_back = (
        dot(act_panel, columns(grad_panel, o), 0, 0).astype(BF16) for o in (1, 3)
    )
    in_ahead, in_back, out_ahead, out_back = lax.optimization_barrier(
        (in_ahead, in_back, out_ahead, out_back)
    )
    up, down = phase((part(3) + up, "z", -1), (part(6) + down, "z", 1))
    in_up, out_up = phase((in_ahead + in_up, "x", -1), (out_ahead + out_up, "y", -1))
    up, down = phase((part(2) + up, "z", -1), (part(7) + down, "z", 1))
    in_down, out_down = phase((in_back, "x", 1), (out_back, "y", 1))
    up, down, in_up, out_up, d_panel, act_panel = lax.optimization_barrier(
        (up, down, in_up, out_up, d_panel, act_panel)
    )
    in_own = dot(columns(normed, 0), d_panel, 0, 0).astype(BF16)
    out_own = dot(act_panel, columns(grad_panel, 0), 0, 0).astype(BF16)
    (up,) = phase((part(1) + up, "z", -1))
    up, down, in_up, out_up, in_down, out_down, in_own, out_own = lax.optimization_barrier(
        (up, down, in_up, out_up, in_down, out_down, in_own, out_own)
    )
    scaled, *pieces = small_call(
        backward_sums,
        [((count, wide), F32)] + [((count, width + 128), BF16)] * RING,
        part(0),
        up,
        down,
        own,
        gain,
        stats,
    )
    arrived = exchange4(pieces, "y")
    scaled, out_own, out_up, out_down = lax.optimization_barrier(
        (scaled, out_own, out_up, out_down)
    )
    grad_w_out = add_up((out_own, out_up, out_down)).astype(BF16)
    through = small_call(
        functools.partial(backward_norm, features, group),
        [((count, width), BF16)] * RING,
        scaled,
        own,
        stats,
        *arrived,
    )
    *through, in_own, in_up, in_down = lax.optimization_barrier(
        (*through, in_own, in_up, in_down)
    )
    grad_w_in = add_up((in_own, in_up, in_down)).astype(BF16)
    through = exchange4(through, "x")
    through = jnp.stack([piece.reshape(RING, group, width) for piece in through], axis=0)
    input_gradient = (cotangent.astype(F32) + from_relative(through).astype(F32)).astype(BF16)
    block = jnp.stack([piece[:, :width].reshape(RING, group, width) for piece in arrived], axis=1)
    block_out = (tokens_in.astype(F32) + from_relative(block).astype(F32)).astype(BF16)
    return block_out, input_gradient, grad_w_in, grad_w_out


def solution(mesh):
    return jax.shard_map(
        shards,
        mesh=mesh,
        in_specs=(
            P(("dp", "col"), "row"),
            P("row"),
            P("row", "col"),
            P("col", "row"),
            P(("dp", "col"), "row"),
        ),
        out_specs=(
            P(("dp", "col"), "row"),
            P(("dp", "col"), "row"),
            P("row", ("dp", "col")),
            P("col", ("dp", "row")),
        ),
        check_vma=False,
    )
```

```python
import functools

import jax
import jax.numpy as jnp
from jax import lax
from jax.experimental import pallas as pl
from jax.experimental.pallas import tpu as pltpu
from jax.sharding import PartitionSpec as P

EPS = 1e-06
GELU_C = 0.7978845608028654
RING = 4
DEPTH = 8
BF16 = jnp.bfloat16
F32 = jnp.float32


def gelu_value(pre):
    inner = GELU_C * (pre + 0.044715 * pre * pre * pre)
    return 0.5 * pre * (1.0 + jnp.tanh(inner))


def gelu_slope(pre):
    inner = GELU_C * (pre + 0.044715 * pre * pre * pre)
    tangent = jnp.tanh(inner)
    return 0.5 * (1.0 + tangent) + 0.5 * pre * (1.0 - tangent * tangent) * GELU_C * (
        1.0 + 3.0 * 0.044715 * pre * pre
    )


def dot(left, right, left_dim, right_dim):
    return lax.dot_general(
        left, right, (((left_dim,), (right_dim,)), ((), ())), preferred_element_type=F32
    )


def receive(value, axis, offset):
    if axis == "core":
        return lax.ppermute(value, "dp", [(0, 1), (1, 0)])
    pairs = []
    for core, step in ((0, offset), (1, -offset)):
        if axis == "z":
            pairs += [(2 * ((i + step) % DEPTH) + core, 2 * i + core) for i in range(DEPTH)]
            continue
        for y in range(RING):
            for x in range(RING):
                if axis == "x":
                    source = RING * y + (x + step) % RING
                else:
                    source = RING * ((y + step) % RING) + x
                pairs.append((2 * source + core, 2 * (RING * y + x) + core))
    return lax.ppermute(value, ("col" if axis == "z" else "row", "dp"), pairs)


def phase(*moves, after=()):
    values = lax.optimization_barrier(tuple(move[0] for move in moves) + tuple(after))
    return [receive(value, axis, offset) for value, (_, axis, offset) in zip(values, moves)]


def phase_and(moves, seen):
    values = lax.optimization_barrier(tuple(move[0] for move in moves) + tuple(seen))
    moved = [receive(value, axis, offset) for value, (_, axis, offset) in zip(values, moves)]
    return moved + list(values[len(moves) :])


def add_up(values):
    total = values[0].astype(F32)
    for value in values[1:]:
        total = total + value.astype(F32)
    return total


def split3(value):
    high = lax.reduce_precision(value, 8, 7)
    middle = lax.reduce_precision(value - high, 8, 7)
    return [part.astype(BF16) for part in (high, middle, value - high - middle)]


def with_row(piece, row):
    filler = jnp.zeros((16 - row.shape[0], row.shape[1]), BF16)
    return jnp.concatenate([piece, row, filler], axis=0)


def sum_columns(first, second):
    lane = lax.broadcasted_iota(jnp.int32, (first.shape[0], 128), 1)
    extra = jnp.zeros(lane.shape, F32)
    for index, part in enumerate(split3(first) + split3(second)):
        extra = jnp.where(lane == index, part.astype(F32), extra)
    return extra.astype(BF16)


def total_sums(columns_per_device, group):
    first, second = 0.0, 0.0
    for o, extra in enumerate(columns_per_device):
        parts = [extra[:, i : i + 1].astype(F32) for i in range(6)]
        one, two = parts[0] + parts[1] + parts[2], parts[3] + parts[4] + parts[5]
        if o:
            one = jnp.concatenate([one[-o * group :], one[: -o * group]], axis=0)
            two = jnp.concatenate([two[-o * group :], two[: -o * group]], axis=0)
        first, second = first + one, second + two
    return first, second


def small_call(body, outputs, *inputs):
    return pl.pallas_call(
        body,
        out_shape=[jax.ShapeDtypeStruct(shape, dtype) for shape, dtype in outputs],
        in_specs=[pl.BlockSpec(memory_space=pltpu.VMEM)] * len(inputs),
        out_specs=[pl.BlockSpec(memory_space=pltpu.VMEM)] * len(outputs),
        compiler_params=pltpu.CompilerParams(vmem_limit_bytes=32 * 1024 * 1024),
    )(*inputs)


def forward_sums(x0, x1, x2, x3, g0, g1, g2, g3, own, gain, s0, s1, s2, s3):
    count, width = g0.shape
    first, second = 0.0, 0.0
    for o, piece in enumerate((x0, x1, x2, x3)):
        block = piece[:count, :]
        own[:, o * width : (o + 1) * width] = block
        rows = piece[count : count + 16, :].astype(F32)
        gain[:, o * width : (o + 1) * width] = rows[0:1] + rows[1:2] + rows[2:3]
        block = block.astype(F32)
        first = first + jnp.sum(block, axis=1, keepdims=True)
        second = second + jnp.sum(block * block, axis=1, keepdims=True)
    extra = sum_columns(first, second)
    for piece, sent in zip((g0, g1, g2, g3), (s0, s1, s2, s3)):
        sent[:, :width] = piece[...]
        sent[:, width:] = extra


def forward_norm(features, group, own, gain, r0, r1, r2, r3, both, stats):
    count, width = own.shape[0], own.shape[1] // RING
    received = (r0, r1, r2, r3)
    first, second = total_sums([piece[:, width:] for piece in received], group)
    mean = first / features
    rstd = lax.rsqrt(second / features - mean * mean + EPS)
    lane = lax.broadcasted_iota(jnp.int32, (count, 128), 1)
    stats[...] = jnp.where(lane == 0, mean, rstd)
    both[:count, :] = ((own[...].astype(F32) - mean) * rstd * gain[...]).astype(BF16)
    for o, piece in enumerate(received):
        both[count:, o * width : (o + 1) * width] = piece[:, :width]


def backward_sums(part, up, down, own, gain, stats, scaled, s0, s1, s2, s3):
    count, width = own.shape[0], own.shape[1] // RING

    def total(rows):
        return part[rows, :].astype(F32) + up[rows, :].astype(F32) + down[rows, :].astype(F32)

    value = total(slice(0, count)) * gain[...]
    scaled[...] = value
    xhat = (own[...].astype(F32) - stats[:, 0:1]) * stats[:, 1:2]
    extra = sum_columns(
        jnp.sum(value, axis=1, keepdims=True), jnp.sum(value * xhat, axis=1, keepdims=True)
    )
    block = total(slice(count, 2 * count)).astype(BF16)
    for o, sent in enumerate((s0, s1, s2, s3)):
        sent[:, :width] = block[:, o * width : (o + 1) * width]
        sent[:, width:] = extra


def backward_norm(features, group, scaled, own, stats, r0, r1, r2, r3, t0, t1, t2, t3):
    width = own.shape[1] // RING
    first, second = total_sums([piece[:, width:] for piece in (r0, r1, r2, r3)], group)
    mean, rstd = stats[:, 0:1], stats[:, 1:2]
    for o, through in enumerate((t0, t1, t2, t3)):
        at = slice(o * width, (o + 1) * width)
        xhat = (own[:, at].astype(F32) - mean) * rstd
        value = scaled[:, at] - first / features - xhat * (second / features)
        through[...] = (rstd * value).astype(BF16)


def exchange4(pieces, axis, after=()):
    first, third, second = lax.optimization_barrier(
        tuple(phase(*[(pieces[RING - o], axis, o) for o in (1, 3, 2)], after=after))
    )
    return [pieces[0], first, second, third]


def rotate(value, axis, start):
    doubled = jnp.concatenate([value, value], axis=axis)
    return lax.dynamic_slice_in_dim(doubled, start, value.shape[axis], axis=axis)


def columns(value, index, width=384):
    return value[:, index * width : (index + 1) * width]


def shards(tokens_in, norm_gain_vector, w_in, w_out, cotangent):
    row = lax.axis_index("row")
    x_at, y_at, core = row % RING, row // RING, lax.axis_index("dp")
    width = tokens_in.shape[1]
    features = width * RING * RING
    group = tokens_in.shape[0] // 16
    rows = DEPTH * group

    x_start = jnp.where(core == 0, x_at, RING - 1 - x_at)
    y_start = jnp.where(core == 0, y_at, RING - 1 - y_at)
    x_back = jnp.where(core == 0, (RING - x_at) % RING, RING - 1 - x_at)
    y_back = jnp.where(core == 0, (RING - y_at) % RING, RING - 1 - y_at)

    def mirrored(value):
        return jnp.where(core == 0, value, value[::-1, ::-1])

    def to_relative(value):
        value = mirrored(value.reshape(RING, RING, group, width))
        return rotate(rotate(value, 0, x_start), 1, y_start)

    def from_relative(value):
        value = rotate(rotate(mirrored(value), 0, x_back), 1, y_back)
        return value.reshape(RING * RING * group, width)

    tokens = to_relative(tokens_in)
    grads = to_relative(cotangent)
    gain_rows = jnp.stack(split3(norm_gain_vector))
    arrived = exchange4(
        [with_row(tokens[o].reshape(RING * group, width), gain_rows) for o in range(RING)], "x"
    )
    count, wide = RING * group, RING * width
    pieces = [grads[:, o].reshape(count, width) for o in range(RING)]
    own, gain, *pieces = small_call(
        forward_sums,
        [((count, wide), BF16), ((1, wide), F32)] + [((count, width + 128), BF16)] * RING,
        *arrived,
        *pieces,
    )
    arrived = exchange4(pieces, "y")
    both, stats = small_call(
        functools.partial(forward_norm, features, group),
        [((2 * count, wide), BF16), ((count, 128), F32)],
        own,
        gain,
        *arrived,
    )

    gathered = [both] + [None] * (DEPTH - 1)
    in_up, out_up, up, down = phase(
        (w_in, "x", 1), (w_out, "y", 1), (both, "z", 1), (both, "z", -1)
    )
    gathered[1], gathered[7] = up, down
    up, down = phase((up, "z", 1), (down, "z", -1))
    gathered[2], gathered[6] = up, down
    up, down, in_up, out_up = lax.optimization_barrier((up, down, in_up, out_up))
    half = w_in.shape[0] // 2
    in_half = lax.dynamic_slice_in_dim(in_up, core * half, half, axis=0)
    half = w_out.shape[0] // 2
    out_half = lax.dynamic_slice_in_dim(out_up, core * half, half, axis=0)
    in_half, out_half, up, down = phase(
        (in_half, "x", 1), (out_half, "y", 1), (up, "z", 1), (down, "z", -1)
    )
    gathered[3], gathered[5] = up, down
    in_half, out_half, up = lax.optimization_barrier((in_half, out_half, up))
    in_down, out_down, in_far, out_far, gathered[4] = phase(
        (in_up, "core", 1),
        (out_up, "core", 1),
        (in_half, "core", 1),
        (out_half, "core", 1),
        (up, "z", 1),
    )

    def panel_of(pieces):
        stacked = jnp.stack([piece.reshape(RING, group, wide) for piece in pieces], axis=1)
        return stacked.reshape(RING * rows, wide)

    normed = panel_of([piece[:count] for piece in gathered])
    grad_panel = panel_of([piece[count:] for piece in gathered])

    def panel_of_weights(block, up, half, down, far, stack):
        block, up = lax.optimization_barrier((block, up))
        size, rows_half = block.shape[stack], half.shape[0]
        shape = [block.shape[0], block.shape[1]]
        shape[stack] *= RING
        panel = jnp.zeros(shape, block.dtype)
        for o, piece, row in (
            (0, block, 0),
            (1, up, 0),
            (2, half, core * rows_half),
            (3, down, 0),
            (2, far, (1 - core) * rows_half),
        ):
            at = (row + o * size, 0) if stack == 0 else (row, o * size)
            panel = lax.dynamic_update_slice(panel, piece, at)
        return panel

    in_panel = panel_of_weights(w_in, in_up, in_half, in_down, in_far, 0)
    out_panel = panel_of_weights(w_out, out_up, out_half, out_down, out_far, 1)
    in_panel, normed = lax.optimization_barrier((in_panel, normed))
    out_panel, grad_panel = lax.optimization_barrier((out_panel, grad_panel))

    def by_group(part):
        return [part[o * rows : (o + 1) * rows] for o in range(RING)]

    pre_shares = by_group(dot(normed, in_panel, 1, 0).astype(BF16))
    d_shares = by_group(dot(grad_panel, out_panel, 1, 1).astype(BF16))
    pre = add_up(exchange4(pre_shares, "y"))
    d_parts = exchange4(d_shares, "x")
    act, pre = lax.optimization_barrier((gelu_value(pre).astype(BF16), pre))
    act_parts = phase((act, "x", 1), (act, "x", 2), (act, "x", 3))
    d_pre = (add_up(d_parts) * gelu_slope(pre)).astype(BF16)
    d_panel = jnp.concatenate(exchange4([d_pre] * RING, "y"), axis=0)
    act_panel = jnp.concatenate([act, *act_parts], axis=0)

    in_far = dot(columns(normed, 2), d_panel, 0, 0).astype(BF16)
    out_far = dot(act_panel, columns(grad_panel, 2), 0, 0).astype(BF16)
    in_up, out_up = phase((in_far, "x", -1), (out_far, "y", -1))
    d_panel, act_panel, in_far, out_far = lax.optimization_barrier(
        (d_panel, act_panel, in_far, out_far)
    )
    dn_part = dot(d_panel, in_panel, 1, 1).astype(BF16).reshape(RING, DEPTH, group, wide)
    out_part = dot(act_panel, out_panel, 1, 0).astype(BF16).reshape(RING, DEPTH, group, wide)

    def part(o):
        return jnp.concatenate(
            [dn_part[:, o].reshape(count, wide), out_part[:, o].reshape(count, wide)], axis=0
        )

    up, down = phase((part(4), "z", -1), (part(5), "z", 1))
    up, down, d_panel, act_panel = lax.optimization_barrier((up, down, d_panel, act_panel))
    in_ahead, in_back = (dot(columns(normed, o), d_panel, 0, 0).astype(BF16) for o in (1, 3))
    out_ahead, out_back = (
        dot(act_panel, columns(grad_panel, o), 0, 0).astype(BF16) for o in (1, 3)
    )
    in_ahead, in_back, out_ahead, out_back = lax.optimization_barrier(
        (in_ahead, in_back, out_ahead, out_back)
    )
    up, down = phase((part(3) + up, "z", -1), (part(6) + down, "z", 1))
    in_down, out_down = phase((in_back, "x", 1), (out_back, "y", 1))
    in_up, out_up = phase((in_ahead + in_up, "x", -1), (out_ahead + out_up, "y", -1))
    up, down = phase((part(2) + up, "z", -1), (part(7) + down, "z", 1))
    up, down, d_panel, act_panel, in_down, out_down = lax.optimization_barrier(
        (up, down, d_panel, act_panel, in_down, out_down)
    )
    in_own = dot(columns(normed, 0), d_panel, 0, 0).astype(BF16)
    out_own = dot(act_panel, columns(grad_panel, 0), 0, 0).astype(BF16)
    (up,) = phase((part(1) + up, "z", -1))
    up, down, in_up, out_up, in_down, out_down, in_own, out_own = lax.optimization_barrier(
        (up, down, in_up, out_up, in_down, out_down, in_own, out_own)
    )
    scaled, *pieces = small_call(
        backward_sums,
        [((count, wide), F32)] + [((count, width + 128), BF16)] * RING,
        part(0),
        up,
        down,
        own,
        gain,
        stats,
    )
    arrived = exchange4(pieces, "y")
    scaled, out_own, out_up, out_down = lax.optimization_barrier(
        (scaled, out_own, out_up, out_down)
    )
    grad_w_out = add_up((out_own, out_up, out_down)).astype(BF16)
    through = small_call(
        functools.partial(backward_norm, features, group),
        [((count, width), BF16)] * RING,
        scaled,
        own,
        stats,
        *arrived,
    )
    *through, in_own, in_up, in_down = lax.optimization_barrier(
        (*through, in_own, in_up, in_down)
    )
    grad_w_in = add_up((in_own, in_up, in_down)).astype(BF16)
    through = exchange4(through, "x")
    through = jnp.stack([piece.reshape(RING, group, width) for piece in through], axis=0)
    input_gradient = (cotangent.astype(F32) + from_relative(through).astype(F32)).astype(BF16)
    block = jnp.stack([piece[:, :width].reshape(RING, group, width) for piece in arrived], axis=1)
    block_out = (tokens_in.astype(F32) + from_relative(block).astype(F32)).astype(BF16)
    return block_out, input_gradient, grad_w_in, grad_w_out


def solution(mesh):
    return jax.shard_map(
        shards,
        mesh=mesh,
        in_specs=(
            P(("dp", "col"), "row"),
            P("row"),
            P("row", "col"),
            P("col", "row"),
            P(("dp", "col"), "row"),
        ),
        out_specs=(
            P(("dp", "col"), "row"),
            P(("dp", "col"), "row"),
            P("row", ("dp", "col")),
            P("col", ("dp", "row")),
        ),
        check_vma=False,
    )
```
